32 devices in a mesh: context: 8 (over z, x), mp: 4 (over y, core).
Axes of the slice: x: 2, y: 2, z: 4, core: 2. Of those that a mesh axis runs over, the one named last changes fastest.
Arguments:
- queries: bfloat16 [8192, 2048], P('context', 'mp'), may hold values from -32 to 32
- keys: bfloat16 [8192, 1024], P('context', 'mp'), may hold values from -32 to 32
- values: bfloat16 [8192, 1024], P('context', 'mp'), may hold values from -6 to 6
- out_grad: bfloat16 [8192, 5376], P(('context', 'mp')), may hold values from -6 to 6
- out_weight: bfloat16 [5376, 2048], P(None, 'mp'), may hold values from -0.125 to 0.125
Outputs:
- query_grad: bfloat16 [8192, 2048], P('context', 'mp')
- key_grad: bfloat16 [8192, 1024], P('context', 'mp')
- value_grad: bfloat16 [8192, 1024], P('context', 'mp')
- weight_grad: bfloat16 [5376, 2048], P('context', 'mp')
The draws below stay inside these ranges and needn't reach their ends.
All inputs are finite; a program needn't handle non-finite values.
Results may differ from the reference program's by a relative error of at most 0.02.
Values may be sent and summed in bfloat16 or wider, within the bound.
No kernel may reach another device: no remote copies, remote signals or barrier semaphores. Data moves between devices by JAX's collectives and lax.ppermute only.
A program may use at most 128 MiB of HBM per device.

```python
import jax
import jax.numpy as jnp
from jax import lax

D = 5376
QUERY_HEADS = 16
KEY_VALUE_HEADS = 8
HEAD_SIZE = 128
WINDOW_KEYS = 512
SEQUENCE_TOKENS = 8192


def draw_queries(key, part):
    drawn_result = jnp.clip(jax.random.normal(jax.random.fold_in(key, 11), (SEQUENCE_TOKENS, QUERY_HEADS * HEAD_SIZE), jnp.float32), -6.0, 6.0)
    return drawn_result.astype(jnp.bfloat16)


def draw_keys(key, part):
    drawn_result = jnp.clip(jax.random.normal(jax.random.fold_in(key, 12), (SEQUENCE_TOKENS, KEY_VALUE_HEADS * HEAD_SIZE), jnp.float32), -6.0, 6.0)
    return drawn_result.astype(jnp.bfloat16)


def strengthened(drawn, rng, source, target, shards_of, factor):
    def block_of(dim):
        return (jnp.arange(drawn.shape[dim]) // (drawn.shape[dim] // shards_of)).reshape((-1,) + (1,) * (drawn.ndim - 1 - dim))

    first = jax.random.permutation(rng, shards_of)[block_of(target)]
    second = (block_of(target) + shards_of // 2) % shards_of
    return jnp.where((block_of(source) == first) | (block_of(source) == second), factor * drawn, drawn)


def levels(key, dims, shards, smallest, top_value):
    factor_of, own = 1.0, jax.random.fold_in(key, 6)
    for dim, shards_of in shards:
        heights = jnp.exp(jax.random.uniform(jax.random.fold_in(own, dim), (shards_of,), jnp.float32, smallest / len(shards), top_value / len(shards)))
        factor_of = factor_of * jnp.repeat(heights, dims[dim] // shards_of).reshape([-1 if axis == dim else 1 for axis in range(len(dims))])
    return factor_of


def scatter_about(rng, dims, deviation, bound, pieces=(), held_as=jnp.bfloat16):
    drawn = jax.random.normal(rng, dims, jnp.float32) * deviation
    if len(pieces) > 0:
        drawn = levels(rng, dims, pieces, -0.22, 0.18) * drawn
    return jnp.clip(drawn, min=-bound, max=bound).astype(held_as)


def heavy_noise(own_key, shape, spread, bound, split, heavy, held_as=jnp.bfloat16):
    drawn = spread * jax.random.normal(own_key, shape, jnp.float32)
    if split:
        drawn = drawn * levels(own_key, shape, split, -0.22, 0.18)
    return jnp.clip(strengthened(drawn, jax.random.fold_in(own_key, 3), *heavy), -bound, bound).astype(held_as)


def setup_inputs(seed: int = 0) -> dict:
    arg_keys = jax.random.split(jax.random.key(seed), 6)
    queries = draw_queries(jax.random.fold_in(arg_keys[5], 71), 0)
    keys = draw_keys(jax.random.fold_in(arg_keys[5], 71), 0)
    values = scatter_about(arg_keys[2], (SEQUENCE_TOKENS, KEY_VALUE_HEADS * HEAD_SIZE), 1.0, 6.0, ((0, 8), (1, 4)))
    out_grad = heavy_noise(arg_keys[3], (SEQUENCE_TOKENS, D), 1.0, 6.0, ((0, 32),), (0, 1, 32, 2.75))
    out_weight = scatter_about(arg_keys[4], (D, QUERY_HEADS * HEAD_SIZE), (QUERY_HEADS * HEAD_SIZE) ** -0.5, 0.125, ((1, 4),))
    return dict(queries=queries, keys=keys, values=values, out_grad=out_grad, out_weight=out_weight)


SCALE = 168.0 ** -0.5
NEG = -1.0e30


def band_grads(query_rows_block, key_rows_block, value_rows_block, output_grad_rows, key_start):
    rows = query_rows_block.shape[0]
    span = key_rows_block.shape[0]
    qf = query_rows_block.astype(jnp.float32)
    kf = key_rows_block.astype(jnp.float32)
    vf = value_rows_block.astype(jnp.float32)
    df = output_grad_rows.astype(jnp.float32)
    scores = jnp.einsum("qhgd,khd->hgqk", qf, kf, preferred_element_type=jnp.float32) * SCALE
    qpos = jnp.arange(rows, dtype=jnp.int32)[:, None]
    kpos = jnp.arange(span, dtype=jnp.int32)[None, :]
    allowed = (kpos > qpos) & (kpos <= qpos + (span - rows)) & (kpos + key_start >= 0)
    scores = jnp.where(allowed, scores, NEG)
    top = jnp.max(scores, axis=-1, keepdims=True)
    weights = jnp.exp(scores - top)
    prob = weights / jnp.sum(weights, axis=-1, keepdims=True)
    prob_b = prob.astype(jnp.bfloat16)
    pf = prob_b.astype(jnp.float32)
    attn = jnp.einsum("hgqk,khd->qhgd", pf, vf, preferred_element_type=jnp.float32).astype(jnp.bfloat16)
    delta = jnp.sum(df * attn.astype(jnp.float32), axis=-1)
    delta = jnp.transpose(delta, (1, 2, 0))[..., None]
    dprob = jnp.einsum("qhgd,khd->hgqk", df, vf, preferred_element_type=jnp.float32)
    dscore = (prob * (dprob - delta) * SCALE).astype(jnp.bfloat16).astype(jnp.float32)
    dq = jnp.einsum("hgqk,khd->qhgd", dscore, kf, preferred_element_type=jnp.float32)
    key_gradient = jnp.einsum("hgqk,qhgd->khd", dscore, qf, preferred_element_type=jnp.float32)
    value_gradient = jnp.einsum("hgqk,qhgd->khd", pf, df, preferred_element_type=jnp.float32)
    return dq, attn, key_gradient, value_gradient


def reference(queries, keys, values, out_grad, out_weight):
    query_group = QUERY_HEADS // KEY_VALUE_HEADS
    block_index = WINDOW_KEYS // 2
    output_gradient = jnp.dot(out_grad, out_weight, preferred_element_type=jnp.float32).astype(jnp.bfloat16)
    key_padding = jnp.concatenate([jnp.zeros((WINDOW_KEYS, KEY_VALUE_HEADS * HEAD_SIZE), jnp.bfloat16), keys], 0)
    value_padding = jnp.concatenate([jnp.zeros((WINDOW_KEYS, KEY_VALUE_HEADS * HEAD_SIZE), jnp.bfloat16), values], 0)

    def step(carry, index):
        key_gradient_total, value_gradient_total = carry
        start_position = (index * block_index).astype(jnp.int32)
        query_rows_block = lax.dynamic_slice_in_dim(queries, start_position, block_index, 0).reshape(block_index, KEY_VALUE_HEADS, query_group, HEAD_SIZE)
        output_grad_rows = lax.dynamic_slice_in_dim(output_gradient, start_position, block_index, 0).reshape(block_index, KEY_VALUE_HEADS, query_group, HEAD_SIZE)
        key_rows_block = lax.dynamic_slice_in_dim(key_padding, start_position, WINDOW_KEYS + block_index, 0).reshape(WINDOW_KEYS + block_index, KEY_VALUE_HEADS, HEAD_SIZE)
        value_rows_block = lax.dynamic_slice_in_dim(value_padding, start_position, WINDOW_KEYS + block_index, 0).reshape(WINDOW_KEYS + block_index, KEY_VALUE_HEADS, HEAD_SIZE)
        dq, attn, key_gradient, value_gradient = band_grads(query_rows_block, key_rows_block, value_rows_block, output_grad_rows, start_position - WINDOW_KEYS)
        earlier_keys = lax.dynamic_slice_in_dim(key_gradient_total, start_position, WINDOW_KEYS + block_index, 0)
        earlier_values = lax.dynamic_slice_in_dim(value_gradient_total, start_position, WINDOW_KEYS + block_index, 0)
        key_gradient_total = lax.dynamic_update_slice_in_dim(key_gradient_total, earlier_keys + key_gradient.reshape(WINDOW_KEYS + block_index, KEY_VALUE_HEADS * HEAD_SIZE), start_position, 0)
        value_gradient_total = lax.dynamic_update_slice_in_dim(value_gradient_total, earlier_values + value_gradient.reshape(WINDOW_KEYS + block_index, KEY_VALUE_HEADS * HEAD_SIZE), start_position, 0)
        return (key_gradient_total, value_gradient_total), (dq.reshape(block_index, QUERY_HEADS * HEAD_SIZE).astype(jnp.bfloat16), attn.reshape(block_index, QUERY_HEADS * HEAD_SIZE))

    zero_filled = jnp.zeros((WINDOW_KEYS + SEQUENCE_TOKENS, KEY_VALUE_HEADS * HEAD_SIZE), jnp.float32)
    (key_gradient_total, value_gradient_total), (dq_blocks, attn_blocks) = lax.scan(step, (zero_filled, zero_filled), jnp.arange(SEQUENCE_TOKENS // block_index, dtype=jnp.int32))
    query_grad = dq_blocks.reshape(SEQUENCE_TOKENS, QUERY_HEADS * HEAD_SIZE)
    attn_all = attn_blocks.reshape(SEQUENCE_TOKENS, QUERY_HEADS * HEAD_SIZE)
    key_grad = key_gradient_total[WINDOW_KEYS:].astype(jnp.bfloat16)
    value_grad = value_gradient_total[WINDOW_KEYS:].astype(jnp.bfloat16)
    weight_grad = lax.dot_general(out_grad, attn_all, (((0,), (0,)), ((), ())), preferred_element_type=jnp.float32).astype(jnp.bfloat16)
    return query_grad, key_grad, value_grad, weight_grad
```

```python
import functools

import jax
import jax.numpy as jnp
from jax import lax
from jax.experimental import pallas as pl
from jax.experimental.pallas import tpu as pltpu
from jax.sharding import PartitionSpec as P

HEAD_SIZE = 128
WINDOW_KEYS = 512
SCALE = 168.0 ** (-0.5)
LOG2E = 1.4426950408889634
NEG = -1e30
TILE = WINDOW_KEYS // 2
F32 = jnp.float32
BF16 = jnp.bfloat16
VMEM_LIMIT = 28 * 1024 * 1024


def dot(a, b, contract_a, contract_b):
    return lax.dot_general(
        a, b, (((contract_a,), (contract_b,)), ((), ())), preferred_element_type=F32
    )


def vmem():
    return pl.BlockSpec(memory_space=pltpu.VMEM)


def smem():
    return pl.BlockSpec(memory_space=pltpu.SMEM)


def params():
    return pltpu.CompilerParams(vmem_limit_bytes=VMEM_LIMIT)


def cost(flops, nbytes, trans=0):
    return pl.CostEstimate(flops=flops, bytes_accessed=nbytes, transcendentals=trans)


def gather_columns_kernel(blocks, blk, lens, og_ref, *out_refs):
    off = 0
    for out, length in zip(out_refs, lens):
        out[...] = jnp.concatenate(
            [og_ref[:, t * blk + off : t * blk + off + length] for t in range(blocks)], axis=1
        )
        off += length


def gather_columns(og, blocks, lens):
    rows, width = og.shape
    return pl.pallas_call(
        functools.partial(gather_columns_kernel, blocks, width // blocks, lens),
        out_shape=[jax.ShapeDtypeStruct((rows, blocks * n), BF16) for n in lens],
        in_specs=[vmem()],
        out_specs=[vmem() for _ in lens],
        compiler_params=params(),
        cost_estimate=cost(0, 4 * rows * width),
        name="gather_columns",
    )(og)


def forward_kernel(kv_local, group, first, flag_ref, q_ref, k_ref, v_ref, attn_ref, prob_ref):
    row = lax.broadcasted_iota(jnp.int32, (TILE, TILE), 0)
    col = lax.broadcasted_iota(jnp.int32, (TILE, TILE), 1)
    upper = col > row
    if first:
        has_prev = flag_ref[0] > 0
    for g in range(kv_local):
        gcols = slice(g * HEAD_SIZE, (g + 1) * HEAD_SIZE)
        for i in range(2):
            k = k_ref[i * TILE : i * TILE + 3 * TILE, gcols]
            v = v_ref[i * TILE : i * TILE + 3 * TILE, gcols]
            for h in range(group):
                head = g * group + h
                hcols = slice(head * HEAD_SIZE, (head + 1) * HEAD_SIZE)
                q = q_ref[i * TILE : (i + 1) * TILE, hcols]
                s = dot(q, k, 1, 1)
                s0, s1, s2 = s[:, :TILE], s[:, TILE : 2 * TILE], s[:, 2 * TILE :]
                if first:
                    s0 = jnp.where(has_prev, s0, NEG)
                    if i == 0:
                        s1 = jnp.where(has_prev, s1, NEG)
                edge = jnp.where(upper, s0, s2)
                top = jnp.max(jnp.maximum(edge, s1), axis=1, keepdims=True)
                edge = jnp.exp2((edge - top) * (SCALE * LOG2E))
                mid = jnp.exp2((s1 - top) * (SCALE * LOG2E))
                inv = 1.0 / jnp.sum(edge + mid, axis=1, keepdims=True)
                edge = edge * inv
                p0 = jnp.where(upper, edge, 0.0).astype(BF16)
                p1 = (mid * inv).astype(BF16)
                p2 = jnp.where(upper, 0.0, edge).astype(BF16)
                prob_ref[g, i, h, :, :TILE] = p0
                prob_ref[g, i, h, :, TILE : 2 * TILE] = p1
                prob_ref[g, i, h, :, 2 * TILE :] = p2
                attn = dot(jnp.concatenate([p0, p1, p2], axis=1), v, 1, 0)
                attn_ref[i * TILE : (i + 1) * TILE, hcols] = attn.astype(BF16)


def forward(flag, q, k, v, first):
    rows, width = q.shape
    kv_local = k.shape[1] // HEAD_SIZE
    group = width // k.shape[1]
    return pl.pallas_call(
        functools.partial(forward_kernel, kv_local, group, first),
        out_shape=[
            jax.ShapeDtypeStruct((rows, width), BF16),
            jax.ShapeDtypeStruct((kv_local, 2, group, TILE, 3 * TILE), BF16),
        ],
        in_specs=[smem(), vmem(), vmem(), vmem()],
        out_specs=[vmem(), vmem()],
        compiler_params=params(),
        cost_estimate=cost(16 * rows * width * 3 * TILE, 8 * rows * width),
        name="attention_forward_first" if first else "attention_forward_second",
    )(flag, q, k, v)


def backward_kernel(kv_local, group, first, q_ref, k_ref, v_ref, do_ref, attn_ref, prob_ref, *rest):
    if first:
        dq_ref, halo_ref, own_ref, dk_acc, dv_acc = rest
    else:
        prev_ref, dq_ref, done_ref, own_ref, dk_acc, dv_acc = rest
    kv_width = kv_local * HEAD_SIZE
    for g in range(kv_local):
        gcols = slice(g * HEAD_SIZE, (g + 1) * HEAD_SIZE)
        for i in range(2):
            rows = slice(i * TILE, (i + 1) * TILE)
            span = slice(i * TILE, i * TILE + 3 * TILE)
            k = k_ref[span, gcols]
            v = v_ref[span, gcols]
            dk = jnp.zeros((HEAD_SIZE, 3 * TILE), F32)
            dv = jnp.zeros((HEAD_SIZE, 3 * TILE), F32)
            for h in range(group):
                head = g * group + h
                hcols = slice(head * HEAD_SIZE, (head + 1) * HEAD_SIZE)
                q = q_ref[rows, hcols]
                do = do_ref[rows, hcols]
                delta = jnp.sum(
                    do.astype(F32) * attn_ref[rows, hcols].astype(F32), axis=1, keepdims=True
                )
                p = prob_ref[g, i, h]
                ds = (p.astype(F32) * (dot(do, v, 1, 1) - delta)).astype(BF16)
                dq_ref[rows, hcols] = (dot(ds, k, 1, 0) * SCALE).astype(BF16)
                dk += dot(q, ds, 0, 0)
                dv += dot(do, p, 0, 0)
            if i == 0:
                dk_acc[:, : 3 * TILE] = dk
                dv_acc[:, : 3 * TILE] = dv
            else:
                dk_acc[:, TILE : 3 * TILE] += dk[:, : 2 * TILE]
                dv_acc[:, TILE : 3 * TILE] += dv[:, : 2 * TILE]
                dk_acc[:, 3 * TILE :] = dk[:, 2 * TILE :]
                dv_acc[:, 3 * TILE :] = dv[:, 2 * TILE :]
        for acc, base, factor in ((dk_acc, 0, SCALE), (dv_acc, kv_width, 1.0)):
            cols = slice(base + g * HEAD_SIZE, base + (g + 1) * HEAD_SIZE)
            low = acc[:, :WINDOW_KEYS].T
            high = acc[:, WINDOW_KEYS:].T
            if factor != 1.0:
                low, high = low * factor, high * factor
            if first:
                halo_ref[:, cols] = low.astype(BF16)
            else:
                done_ref[:, cols] = (low + prev_ref[:, cols]).astype(BF16)
            own_ref[:, cols] = high


def backward(q, k, v, do, attn, prob, prev=None):
    first = prev is None
    rows, width = q.shape
    kv_width = k.shape[1]
    kv_local = kv_width // HEAD_SIZE
    group = width // kv_width
    args = [q, k, v, do, attn, prob] + ([] if first else [prev])
    return pl.pallas_call(
        functools.partial(backward_kernel, kv_local, group, first),
        out_shape=[
            jax.ShapeDtypeStruct((rows, width), BF16),
            jax.ShapeDtypeStruct((WINDOW_KEYS, 2 * kv_width), BF16),
            jax.ShapeDtypeStruct((WINDOW_KEYS, 2 * kv_width), F32),
        ],
        in_specs=[vmem() for _ in args],
        out_specs=[vmem() for _ in range(3)],
        scratch_shapes=[
            pltpu.VMEM((HEAD_SIZE, 4 * TILE), F32),
            pltpu.VMEM((HEAD_SIZE, 4 * TILE), F32),
        ],
        compiler_params=params(),
        cost_estimate=cost(16 * rows * width * 3 * TILE, 8 * rows * width),
        name="attention_backward_first" if first else "attention_backward_second",
    )(*args)


def projection_kernel(peers, blocks, off, length, start, last, place_ref, *refs):
    og_refs = refs[:peers]
    refs = refs[peers:]
    w_ref, attn_ref = refs[:2]
    refs = refs[2:]
    if not start:
        acc_ref, refs = refs[0], refs[1:]
    out_ref, send_ref, keep_ref, w_vmem, part, sem = refs
    copy = pltpu.make_async_copy(w_ref.at[:, pl.ds(off, length), :], w_vmem, sem)
    copy.start()
    mine, context = place_ref[0], place_ref[1]
    width = attn_ref.shape[2]
    total = blocks * length
    attn = jnp.concatenate([attn_ref[mine ^ r] for r in range(peers)], axis=0)
    step = 256 if total % 256 == 0 else 128
    for s in range(0, total, step):
        og = jnp.concatenate([og_ref[:, s : s + step] for og_ref in og_refs], axis=0)
        part[s : s + step, :] = dot(og, attn, 0, 0)
    for i in range(blocks // 2):
        target = (2 * i) ^ context
        at = pl.multiple_of(target * length, 8)
        keep_ref[i] = part[pl.ds(at, length), :].astype(keep_ref.dtype)
        at = pl.multiple_of((target ^ 1) * length, 8)
        send_ref[i] = part[pl.ds(at, length), :].astype(BF16)
    copy.wait()
    w = w_vmem[...].reshape(total, width)
    for r in range(peers):
        out = dot(og_refs[r][...], w, 1, 0)
        if not start:
            out = out + acc_ref[r]
        if last:
            out_ref[mine ^ r] = out.astype(BF16)
        else:
            out_ref[r] = out


def projection(place, ogs, w, attn, acc, blocks, off, length, last):
    peers = len(ogs)
    rows, total = ogs[0].shape
    width = attn.shape[2]
    start = acc is None
    args = [place, *ogs, w, attn] + ([] if start else [acc])
    specs = [smem()] + [vmem()] * peers + [pl.BlockSpec(memory_space=pl.ANY), vmem()]
    specs += [] if start else [vmem()]
    half = jax.ShapeDtypeStruct((blocks // 2, length, width), BF16)
    return pl.pallas_call(
        functools.partial(projection_kernel, peers, blocks, off, length, start, last),
        out_shape=[
            jax.ShapeDtypeStruct((peers, rows, width), BF16 if last else F32),
            half,
            half,
        ],
        in_specs=specs,
        out_specs=[vmem()] * 3,
        scratch_shapes=[
            pltpu.VMEM((blocks, length, width), BF16),
            pltpu.VMEM((total, width), F32),
            pltpu.SemaphoreType.DMA,
        ],
        compiler_params=params(),
        cost_estimate=cost(4 * peers * rows * total * width, 4 * rows * peers * total),
        name="projection",
    )(*args)


def chunk_lengths(blk):
    if blk == 672:
        return (224, 192, 160, 96)
    return (blk,)


def exchange(x, axis, by):
    return lax.ppermute(x, axis, [(i, i ^ by) for i in range(lax.axis_size(axis))])


def shards(queries, keys, values, out_grad, out_weight):
    shard, width = queries.shape
    kv_width = keys.shape[1]
    contexts = lax.axis_size("context")
    peers = lax.axis_size("mp")
    context = lax.axis_index("context")
    mine = lax.axis_index("mp")
    blk = out_weight.shape[0] // contexts
    lens = chunk_lengths(blk)
    half = WINDOW_KEYS

    halo = jnp.concatenate([keys[shard - half :], values[shard - half :]], axis=1)
    halo = lax.ppermute(halo, "context", [(i, i + 1) for i in range(contexts - 1)])
    if len(lens) == 1:
        own = [out_grad]
    else:
        own = gather_columns(out_grad, contexts, lens)
    gathered = []
    for og in own:
        parts = [og, exchange(og, "mp", 1)]
        for by in range(2, peers, 2):
            far = exchange(og, "mp", by)
            parts += [far, exchange(far, "mp", 1)]
        gathered.append(parts)

    flag = context.reshape(1).astype(jnp.int32)
    place = jnp.stack([mine, context]).astype(jnp.int32)
    attn_high, prob_high = forward(flag, queries[half:], keys, values, False)
    key_window = jnp.concatenate([halo[:, :kv_width], keys[:half]], axis=0)
    value_window = jnp.concatenate([halo[:, kv_width:], values[:half]], axis=0)
    attn_low, prob_low = forward(flag, queries[:half], key_window, value_window, True)
    attn = jnp.concatenate([attn_low, attn_high], axis=0).reshape(peers, shard // peers, width)

    weight = out_weight.reshape(contexts, blk, width)
    acc, off, reduced = None, 0, []
    for j, length in enumerate(lens):
        acc, send, keep = projection(
            place, gathered[j], weight, attn, acc, contexts, off, length, j == len(lens) - 1
        )
        off += length
        by, count = 1, contexts // 2
        order = list(range(count))
        keep = keep.astype(F32)
        while True:
            keep = keep + exchange(send, "context", by).astype(F32)
            if count == 1:
                break
            by, count = by * 2, count // 2
            send, keep = keep[1::2].astype(BF16), keep[0::2]
        reduced.append(keep[0])
    weight_grad = jnp.concatenate(reduced, axis=0).astype(BF16)

    dout = acc.reshape(shard, width)
    dq_low, halo_grad, own_low = backward(
        queries[:half], key_window, value_window, dout[:half], attn_low, prob_low
    )
    halo_grad = lax.ppermute(halo_grad, "context", [(i + 1, i) for i in range(contexts - 1)])
    dq_high, done, own_high = backward(
        queries[half:], keys, values, dout[half:], attn_high, prob_high, own_low
    )
    own_high = (own_high + halo_grad.astype(F32)).astype(BF16)
    query_grad = jnp.concatenate([dq_low, dq_high], axis=0)
    kv_grad = jnp.concatenate([done, own_high], axis=0)
    return query_grad, kv_grad[:, :kv_width], kv_grad[:, kv_width:], weight_grad


def solution(mesh):
    return jax.shard_map(
        shards,
        mesh=mesh,
        in_specs=(
            P("context", "mp"),
            P("context", "mp"),
            P("context", "mp"),
            P(("context", "mp"), None),
            P(None, "mp"),
        ),
        out_specs=(P("context", "mp"), P("context", "mp"), P("context", "mp"), P("context", "mp")),
        check_vma=False,
    )
```

```python
import functools

import jax
import jax.numpy as jnp
from jax import lax
from jax.experimental import pallas as pl
from jax.experimental.pallas import tpu as pltpu
from jax.sharding import PartitionSpec as P

HEAD_SIZE = 128
WINDOW_KEYS = 512
SCALE = 168.0 ** (-0.5)
LOG2E = 1.4426950408889634
NEG = -1e30
TILE = WINDOW_KEYS // 2
LAGS = (1, 2, 3, 4, 5)
TAIL_ONE = True


def TAIL(item):
    return (item[0] + item[1], item[0])


LENS = (160, 144, 128, 112, 80, 48)
SWAP = (0, 0, 0, 0, 0, 0)
PIECES = (1, 1, 1, 1, 1, 1)
AHEAD = 1
AHEAD_FROM = 0
COST = None
F32 = jnp.float32
BF16 = jnp.bfloat16
VMEM_LIMIT = 8 * 1024 * 1024


def dot(a, b, contract_a, contract_b):
    return lax.dot_general(
        a, b, (((contract_a,), (contract_b,)), ((), ())), preferred_element_type=F32
    )


def vmem():
    return pl.BlockSpec(memory_space=pltpu.VMEM)


def hbm():
    return pl.BlockSpec(memory_space=pltpu.HBM)


def params(times=1):
    return pltpu.CompilerParams(vmem_limit_bytes=times * VMEM_LIMIT)


def cost(flops, nbytes, trans=0):
    return COST


def prepare_kernel(blocks, blk, lens, og_ref, *refs):
    off = 0
    for out, length in zip(refs, lens):
        out[...] = jnp.concatenate(
            [og_ref[:, t * blk + off : t * blk + off + length] for t in range(blocks)], axis=1
        )
        off += length


def prepare(og, blocks, lens):
    rows, width = og.shape
    return pl.pallas_call(
        functools.partial(prepare_kernel, blocks, width // blocks, lens),
        out_shape=[jax.ShapeDtypeStruct((rows, blocks * n), BF16) for n in lens],
        in_specs=[vmem()],
        out_specs=[vmem() for _ in lens],
        compiler_params=params(),
        cost_estimate=cost(0, 4 * rows * width),
        name="gather_columns",
    )(og)


def pack_kernel(k_ref, v_ref, out_ref):
    rows = k_ref.shape[0]
    out_ref[0] = k_ref[rows - WINDOW_KEYS :, :]
    out_ref[1] = v_ref[rows - WINDOW_KEYS :, :]


def pack(keys, values):
    return pl.pallas_call(
        pack_kernel,
        out_shape=jax.ShapeDtypeStruct((2, WINDOW_KEYS, keys.shape[1]), BF16),
        in_specs=[vmem(), vmem()],
        out_specs=vmem(),
        compiler_params=params(),
        cost_estimate=cost(0, 8 * WINDOW_KEYS * keys.shape[1]),
        name="pack_halo",
    )(keys, values)


def window(first, i, g, which, prev_ref, own_ref):
    cols = slice(g * HEAD_SIZE, (g + 1) * HEAD_SIZE)
    start = i * TILE
    if not first:
        return own_ref[start : start + 3 * TILE, cols]
    low = prev_ref[which, start:, cols]
    return jnp.concatenate([low, own_ref[: start + TILE, cols]], axis=0)


def forward_kernel(kv_local, group, first, *refs):
    if first:
        q_ref, k_ref, v_ref, prev_ref, attn_ref, prob_ref = refs
        has_prev = lax.axis_index("context") > 0
        base = 0
    else:
        q_ref, k_ref, v_ref, attn_ref, prob_ref = refs
        prev_ref = None
        base = q_ref.shape[0] - WINDOW_KEYS
    row = lax.broadcasted_iota(jnp.int32, (TILE, TILE), 0)
    col = lax.broadcasted_iota(jnp.int32, (TILE, TILE), 1)
    upper = col > row
    for g in range(kv_local):
        for i in range(2):
            k = window(first, i, g, 0, prev_ref, k_ref)
            v = window(first, i, g, 1, prev_ref, v_ref)
            for h in range(group):
                head = g * group + h
                hcols = slice(head * HEAD_SIZE, (head + 1) * HEAD_SIZE)
                q = q_ref[base + i * TILE : base + (i + 1) * TILE, hcols]
                s = dot(q, k, 1, 1)
                s0, s1, s2 = s[:, :TILE], s[:, TILE : 2 * TILE], s[:, 2 * TILE :]
                if first:
                    s0 = jnp.where(has_prev, s0, NEG)
                    if i == 0:
                        s1 = jnp.where(has_prev, s1, NEG)
                edge = jnp.where(upper, s0, s2)
                top = jnp.max(jnp.maximum(edge, s1), axis=1, keepdims=True)
                edge = jnp.exp2((edge - top) * (SCALE * LOG2E))
                mid = jnp.exp2((s1 - top) * (SCALE * LOG2E))
                inv = 1.0 / jnp.sum(edge + mid, axis=1, keepdims=True)
                edge = edge * inv
                p0 = jnp.where(upper, edge, 0.0).astype(BF16)
                p1 = (mid * inv).astype(BF16)
                p2 = jnp.where(upper, 0.0, edge).astype(BF16)
                prob_ref[g, i, h, :, :TILE] = p0
                prob_ref[g, i, h, :, TILE : 2 * TILE] = p1
                prob_ref[g, i, h, :, 2 * TILE :] = p2
                attn = dot(jnp.concatenate([p0, p1, p2], axis=1), v, 1, 0)
                attn_ref[i * TILE : (i + 1) * TILE, hcols] = attn.astype(BF16)


def forward(q, k, v, prev=None):
    first = prev is not None
    width = q.shape[1]
    kv_local = k.shape[1] // HEAD_SIZE
    group = width // k.shape[1]
    args = [q, k, v] + ([prev] if first else [])
    return pl.pallas_call(
        functools.partial(forward_kernel, kv_local, group, first),
        out_shape=[
            jax.ShapeDtypeStruct((WINDOW_KEYS, width), BF16),
            jax.ShapeDtypeStruct((kv_local, 2, group, TILE, 3 * TILE), BF16),
        ],
        in_specs=[vmem() for _ in args],
        out_specs=[vmem(), vmem()],
        compiler_params=params(),
        cost_estimate=cost(16 * WINDOW_KEYS * width * 3 * TILE, 8 * WINDOW_KEYS * width),
        name="attention_forward_first" if first else "attention_forward_second",
    )(*args)


def backward_kernel(kv_local, group, first, *refs):
    q_ref, k_ref, v_ref, do_ref, attn_ref, prob_ref = refs[:6]
    if first:
        prev_ref, dq_ref, halo_ref, own_ref, dk_acc, dv_acc = refs[6:]
        base = 0
    else:
        low_ref, dq_ref, done_ref, own_ref, dk_acc, dv_acc = refs[6:]
        prev_ref = None
        base = q_ref.shape[0] - WINDOW_KEYS
    for g in range(kv_local):
        for i in range(2):
            rows = slice(i * TILE, (i + 1) * TILE)
            wide_rows = slice(base + i * TILE, base + (i + 1) * TILE)
            k = window(first, i, g, 0, prev_ref, k_ref)
            v = window(first, i, g, 1, prev_ref, v_ref)
            dk = jnp.zeros((HEAD_SIZE, 3 * TILE), F32)
            dv = jnp.zeros((HEAD_SIZE, 3 * TILE), F32)
            for h in range(group):
                head = g * group + h
                hcols = slice(head * HEAD_SIZE, (head + 1) * HEAD_SIZE)
                q = q_ref[wide_rows, hcols]
                do = do_ref[wide_rows, hcols]
                delta = jnp.sum(
                    do.astype(F32) * attn_ref[rows, hcols].astype(F32), axis=1, keepdims=True
                )
                p = prob_ref[g, i, h]
                ds = (p.astype(F32) * (dot(do, v, 1, 1) - delta)).astype(BF16)
                dq_ref[rows, hcols] = (dot(ds, k, 1, 0) * SCALE).astype(BF16)
                dk += dot(q, ds, 0, 0)
                dv += dot(do, p, 0, 0)
            if i == 0:
                dk_acc[:, : 3 * TILE] = dk
                dv_acc[:, : 3 * TILE] = dv
            else:
                dk_acc[:, TILE : 3 * TILE] += dk[:, : 2 * TILE]
                dv_acc[:, TILE : 3 * TILE] += dv[:, : 2 * TILE]
                dk_acc[:, 3 * TILE :] = dk[:, 2 * TILE :]
                dv_acc[:, 3 * TILE :] = dv[:, 2 * TILE :]
        cols = slice(g * HEAD_SIZE, (g + 1) * HEAD_SIZE)
        for which, acc, factor in ((0, dk_acc, SCALE), (1, dv_acc, 1.0)):
            low = acc[:, :WINDOW_KEYS].T
            high = acc[:, WINDOW_KEYS:].T
            if factor != 1.0:
                low, high = low * factor, high * factor
            if first:
                halo_ref[which, :, cols] = low.astype(BF16)
            else:
                done_ref[which, :, cols] = (low + low_ref[which, :, cols]).astype(BF16)
            own_ref[which, :, cols] = high


def backward(q, k, v, do, attn, prob, prev=None, low=None):
    first = prev is not None
    width = q.shape[1]
    kv_width = k.shape[1]
    args = [q, k, v, do, attn, prob, prev if first else low]
    return pl.pallas_call(
        functools.partial(backward_kernel, kv_width // HEAD_SIZE, width // kv_width, first),
        out_shape=[
            jax.ShapeDtypeStruct((WINDOW_KEYS, width), BF16),
            jax.ShapeDtypeStruct((2, WINDOW_KEYS, kv_width), BF16),
            jax.ShapeDtypeStruct((2, WINDOW_KEYS, kv_width), F32),
        ],
        in_specs=[vmem() for _ in args],
        out_specs=[vmem() for _ in range(3)],
        scratch_shapes=[
            pltpu.VMEM((HEAD_SIZE, 4 * TILE), F32),
            pltpu.VMEM((HEAD_SIZE, 4 * TILE), F32),
        ],
        compiler_params=params(),
        cost_estimate=cost(16 * WINDOW_KEYS * width * 3 * TILE, 8 * WINDOW_KEYS * width),
        name="attention_backward_first" if first else "attention_backward_second",
    )(*args)


def join_kernel(done_ref, own_ref, got_ref, dk_ref, dv_ref):
    for which, out in ((0, dk_ref), (1, dv_ref)):
        rows = out.shape[0]
        out[: rows - WINDOW_KEYS, :] = done_ref[which]
        high = own_ref[which] + got_ref[which].astype(F32)
        out[rows - WINDOW_KEYS :, :] = high.astype(BF16)


def join(done, own, got, rows):
    shape = jax.ShapeDtypeStruct((rows, own.shape[2]), BF16)
    return pl.pallas_call(
        join_kernel,
        out_shape=[shape, shape],
        in_specs=[vmem()] * 3,
        out_specs=[vmem()] * 2,
        compiler_params=params(),
        cost_estimate=cost(0, 12 * WINDOW_KEYS * own.shape[2]),
        name="join_gradients",
    )(done, own, got)


def concat_kernel(low_ref, high_ref, out_ref):
    rows = low_ref.shape[0]
    out_ref[:rows, :] = low_ref[...]
    out_ref[rows:, :] = high_ref[...]


def concat(low, high):
    return pl.pallas_call(
        concat_kernel,
        out_shape=jax.ShapeDtypeStruct((2 * low.shape[0], low.shape[1]), BF16),
        in_specs=[vmem()] * 2,
        out_specs=vmem(),
        compiler_params=params(),
        cost_estimate=cost(0, 4 * low.shape[0] * low.shape[1]),
        name="join_halves",
    )(low, high)


def add_kernel(keep_ref, *refs):
    count, length = keep_ref.shape[:2]
    pieces = len(refs) - (1 if count == 1 else 2)
    got_refs, out_refs = refs[:pieces], refs[pieces:]
    size = length // pieces
    for i in range(count):
        for p, got_ref in enumerate(got_refs):
            rows = slice(p * size, (p + 1) * size)
            total = keep_ref[i, rows, :].astype(F32) + got_ref[i].astype(F32)
            if count == 1:
                out_refs[0][rows, :] = total.astype(BF16)
            else:
                out = out_refs[i % 2]
                out[i // 2, rows, :] = total.astype(out.dtype)


def add(keep, got):
    count, length, width = keep.shape
    if count == 1:
        out_shape = [jax.ShapeDtypeStruct((length, width), BF16)]
    else:
        half = (count // 2, length, width)
        out_shape = [jax.ShapeDtypeStruct(half, F32), jax.ShapeDtypeStruct(half, BF16)]
    return pl.pallas_call(
        add_kernel,
        out_shape=out_shape,
        in_specs=[vmem()] * (1 + len(got)),
        out_specs=[vmem() for _ in out_shape],
        compiler_params=params(),
        cost_estimate=cost(0, 8 * count * length * width),
        name="add_partials",
    )(keep, *got)


def projection_kernel(peers, blocks, off, length, start, last, bits, pieces, *refs):
    og_refs = refs[:peers]
    w_ref, low_ref, high_ref = refs[peers : peers + 3]
    refs = refs[peers + 3 :]
    if not start:
        acc_ref, refs = refs[0], refs[1:]
    out_ref, keep_ref = refs[:2]
    send_refs = refs[2 : 2 + pieces]
    w_vmem, attn_all, part, sem = refs[2 + pieces :]
    copy = pltpu.make_async_copy(w_ref.at[:, pl.ds(off, length), :], w_vmem, sem)
    copy.start()
    mine, context = lax.axis_index("mp"), lax.axis_index("context")
    rows, width = og_refs[0].shape[0], low_ref.shape[1]
    total = blocks * length
    for r in range(peers // 2):
        attn_all[r] = low_ref[r * rows : (r + 1) * rows, :]
        attn_all[r + peers // 2] = high_ref[r * rows : (r + 1) * rows, :]
    attn = jnp.concatenate([attn_all[mine ^ r] for r in range(peers)], axis=0)
    step = 256 if total % 256 == 0 else 128
    for s in range(0, total, step):
        og = jnp.concatenate([og_ref[:, s : s + step] for og_ref in og_refs], axis=0)
        part[s : s + step, :] = dot(og, attn, 0, 0)
    size = length // pieces
    for i in range(blocks // 2):
        target = sum(bit for k, bit in enumerate(bits[1:]) if i >> k & 1) ^ context
        at = pl.multiple_of(target * length, 8)
        keep_ref[i] = part[pl.ds(at, length), :].astype(keep_ref.dtype)
        for p, send_ref in enumerate(send_refs):
            at = pl.multiple_of((target ^ bits[0]) * length + p * size, 8)
            send_ref[i] = part[pl.ds(at, size), :].astype(BF16)
    copy.wait()
    w = w_vmem[...].reshape(total, width)
    for r in range(peers):
        out = dot(og_refs[r][...], w, 1, 0)
        if not start:
            out = out + acc_ref[r]
        if last:
            out_ref[mine ^ r] = out.astype(BF16)
        else:
            out_ref[r] = out


def projection(ogs, w, low, high, acc, blocks, off, length, last, bits, pieces):
    peers = len(ogs)
    rows, total = ogs[0].shape
    width = low.shape[1]
    start = acc is None
    args = [*ogs, w, low, high] + ([] if start else [acc])
    specs = [vmem()] * peers + [hbm()] + [vmem()] * (2 if start else 3)
    keep = jax.ShapeDtypeStruct((blocks // 2, length, width), BF16)
    send = jax.ShapeDtypeStruct((blocks // 2, length // pieces, width), BF16)
    return pl.pallas_call(
        functools.partial(
            projection_kernel, peers, blocks, off, length, start, last, bits, pieces
        ),
        out_shape=[
            jax.ShapeDtypeStruct((peers, rows, width), BF16 if last else F32),
            keep,
            *[send] * pieces,
        ],
        in_specs=specs,
        out_specs=[vmem()] * (2 + pieces),
        scratch_shapes=[
            pltpu.VMEM((blocks, length, width), BF16),
            pltpu.VMEM((peers, rows, width), BF16),
            pltpu.VMEM((total, width), F32),
            pltpu.SemaphoreType.DMA,
        ],
        compiler_params=params(4 if start and last else 1),
        cost_estimate=cost(4 * peers * rows * total * width, 4 * rows * peers * total),
        name="projection",
    )(*args)


def chunk_plan(blk, contexts):
    bits = [1 << k for k in range(contexts.bit_length() - 1)]
    if blk != 672:
        return (blk,), (bits,), (1,)
    swapped = [bits[1], bits[0], *bits[2:]]
    return LENS, [swapped if swap else bits for swap in SWAP], PIECES


def exchange(x, axis, by):
    return lax.ppermute(x, axis, [(i, i ^ by) for i in range(lax.axis_size(axis))])


def after(done, x):
    return lax.optimization_barrier((x, done))[0]


def shards(queries, keys, values, out_grad, out_weight):
    shard, width = queries.shape
    contexts = lax.axis_size("context")
    peers = lax.axis_size("mp")
    blk = out_weight.shape[0] // contexts
    lens, orders, pieces = chunk_plan(blk, contexts)
    chunks = len(lens)
    weight = out_weight.reshape(contexts, blk, width)

    sibling = exchange(out_grad, "mp", 1)
    own = prepare(out_grad, contexts, lens)
    far = [[exchange(og, "mp", by) for by in range(2, peers, 2)] for og in own]
    halo = pack(after(own[0], keys), values)
    halo = lax.ppermute(halo, "context", [(i, i + 1) for i in range(contexts - 1)])

    attn_high, prob_high = forward(queries, keys, values)
    siblings = prepare(after(attn_high, sibling), contexts, lens)
    halo = after(siblings[0], halo)
    attn_low, prob_low = forward(queries, keys, values, halo)
    done = attn_low

    pending, reduced = [], [None] * chunks

    def reduce_step(item, done):
        chunk, stage, keep, got = item
        got = [after(done, piece) for piece in got]
        if keep.shape[0] == 1:
            reduced[chunk] = add(keep, got)[0]
            return reduced[chunk], None
        keep, send = add(keep, got)
        stage += 1
        return send, (chunk, stage, keep, [exchange(send, "context", orders[chunk][stage])])

    def reduce_round(pending, done):
        later = []
        for item in pending:
            done, item = reduce_step(item, done)
            if item is not None:
                later.append(item)
        return later, done

    def fetch(j, done):
        theirs = [after(done, og) for og in far[j]]
        return theirs, [exchange(og, "mp", 1) for og in theirs], theirs[-1]

    fetched = []
    acc, off = None, 0
    for j, length in enumerate(lens):
        want = min(chunks, j + 1 + (AHEAD if j >= AHEAD_FROM else 0))
        while len(fetched) < want:
            *item, done = fetch(len(fetched), done)
            fetched.append(item)
        theirs, theirs_sibling = fetched[j]
        parts = [own[j], after(done, siblings[j])]
        for og, og_sibling in zip(theirs, theirs_sibling):
            parts += [og, after(done, og_sibling)]
        acc, keep, *send = projection(
            parts, weight, attn_low, attn_high, acc, contexts, off, length, j == chunks - 1,
            orders[j], pieces[j],
        )
        done = acc
        off += length
        got = [exchange(piece, "context", orders[j][0]) for piece in send]
        pending.append((j, 0, keep, got))
        if j < chunks - 1:
            ready = [item for item in pending if item[0] + LAGS[item[1]] <= j]
            rest = [item for item in pending if item[0] + LAGS[item[1]] > j]
            ready, done = reduce_round(ready, done)
            pending = ready + rest

    dout = acc.reshape(shard, width)
    dq_low, halo_grad, own_low = backward(queries, keys, values, dout, attn_low, prob_low, halo)
    halo_grad = lax.ppermute(halo_grad, "context", [(i + 1, i) for i in range(contexts - 1)])
    dq_high, kv_low, own_high = backward(
        queries, keys, values, dout, attn_high, prob_high, low=own_low
    )
    dq = concat(dq_low, dq_high)
    done = own_high
    while pending:
        pending.sort(key=TAIL)
        count = 1 if TAIL_ONE else len(pending)
        ready, done = reduce_round(pending[:count], done)
        pending = ready + pending[count:]
    weight_grad = jnp.concatenate(reduced, axis=0)
    dk, dv = join(kv_low, own_high, halo_grad, shard)
    return dq, dk, dv, weight_grad


def solution(mesh):
    return jax.shard_map(
        shards,
        mesh=mesh,
        in_specs=(
            P("context", "mp"),
            P("context", "mp"),
            P("context", "mp"),
            P(("context", "mp"), None),
            P(None, "mp"),
        ),
        out_specs=(P("context", "mp"), P("context", "mp"), P("context", "mp"), P("context", "mp")),
        check_vma=False,
    )
```

```python
import functools

import jax
import jax.numpy as jnp
from jax import lax
from jax.experimental import pallas as pl
from jax.experimental.pallas import tpu as pltpu
from jax.sharding import PartitionSpec as P

HEAD_SIZE = 128
WINDOW_KEYS = 512
SCALE = 168.0 ** (-0.5)
LOG2E = 1.4426950408889634
NEG = -1e30
TILE = WINDOW_KEYS // 2
LENS = (144, 144, 128, 112, 80, 64)
STEPS = (
    "y0", "y1", "p0", "y2", "p1", "1.0", "y3", "p2", "2.0", "1.1", "y4", "3.0", "p3",
    "2.1", "1.2", "y5", "p4", "p5", "3.1", "1.3", "2.2", "first", "3.2", "2.3", "1.4",
    "second", "1.5", "2.4", "3.3", "2.5", "3.4", "3.5",
)
F32 = jnp.float32
BF16 = jnp.bfloat16
VMEM_LIMIT = 8 * 1024 * 1024


def dot(a, b, contract_a, contract_b):
    return lax.dot_general(
        a, b, (((contract_a,), (contract_b,)), ((), ())), preferred_element_type=F32
    )


def vmem():
    return pl.BlockSpec(memory_space=pltpu.VMEM)


def hbm():
    return pl.BlockSpec(memory_space=pltpu.HBM)


def params(times=1):
    return pltpu.CompilerParams(vmem_limit_bytes=times * VMEM_LIMIT)


def prepare_kernel(blocks, blk, lens, og_ref, *refs):
    off = 0
    for out, length in zip(refs, lens):
        out[...] = jnp.concatenate(
            [og_ref[:, t * blk + off : t * blk + off + length] for t in range(blocks)], axis=1
        )
        off += length


def prepare(og, blocks, lens):
    rows, width = og.shape
    return pl.pallas_call(
        functools.partial(prepare_kernel, blocks, width // blocks, lens),
        out_shape=[jax.ShapeDtypeStruct((rows, blocks * n), BF16) for n in lens],
        in_specs=[vmem()],
        out_specs=[vmem() for _ in lens],
        compiler_params=params(),
        name="gather_columns",
    )(og)


def pack_kernel(k_ref, v_ref, out_ref):
    rows = k_ref.shape[0]
    out_ref[0] = k_ref[rows - WINDOW_KEYS :, :]
    out_ref[1] = v_ref[rows - WINDOW_KEYS :, :]


def pack(keys, values):
    return pl.pallas_call(
        pack_kernel,
        out_shape=jax.ShapeDtypeStruct((2, WINDOW_KEYS, keys.shape[1]), BF16),
        in_specs=[vmem(), vmem()],
        out_specs=vmem(),
        compiler_params=params(),
        name="pack_halo",
    )(keys, values)


def window(first, i, g, which, prev_ref, own_ref):
    cols = slice(g * HEAD_SIZE, (g + 1) * HEAD_SIZE)
    start = i * TILE
    if not first:
        return own_ref[start : start + 3 * TILE, cols]
    low = prev_ref[which, start:, cols]
    return jnp.concatenate([low, own_ref[: start + TILE, cols]], axis=0)


def forward_kernel(kv_local, group, first, *refs):
    if first:
        q_ref, k_ref, v_ref, prev_ref, attn_ref, prob_ref = refs
        has_prev = lax.axis_index("context") > 0
        base = 0
    else:
        q_ref, k_ref, v_ref, attn_ref, prob_ref = refs
        prev_ref = None
        base = q_ref.shape[0] - WINDOW_KEYS
    row = lax.broadcasted_iota(jnp.int32, (TILE, TILE), 0)
    col = lax.broadcasted_iota(jnp.int32, (TILE, TILE), 1)
    upper = col > row
    for g in range(kv_local):
        for i in range(2):
            k = window(first, i, g, 0, prev_ref, k_ref)
            v = window(first, i, g, 1, prev_ref, v_ref)
            for h in range(group):
                head = g * group + h
                hcols = slice(head * HEAD_SIZE, (head + 1) * HEAD_SIZE)
                q = q_ref[base + i * TILE : base + (i + 1) * TILE, hcols]
                s = dot(q, k, 1, 1)
                s0, s1, s2 = s[:, :TILE], s[:, TILE : 2 * TILE], s[:, 2 * TILE :]
                if first:
                    s0 = jnp.where(has_prev, s0, NEG)
                    if i == 0:
                        s1 = jnp.where(has_prev, s1, NEG)
                edge = jnp.where(upper, s0, s2)
                top = jnp.max(jnp.maximum(edge, s1), axis=1, keepdims=True)
                edge = jnp.exp2((edge - top) * (SCALE * LOG2E))
                mid = jnp.exp2((s1 - top) * (SCALE * LOG2E))
                inv = 1.0 / jnp.sum(edge + mid, axis=1, keepdims=True)
                edge = edge * inv
                p0 = jnp.where(upper, edge, 0.0).astype(BF16)
                p1 = (mid * inv).astype(BF16)
                p2 = jnp.where(upper, 0.0, edge).astype(BF16)
                prob_ref[g, i, h, :, :TILE] = p0
                prob_ref[g, i, h, :, TILE : 2 * TILE] = p1
                prob_ref[g, i, h, :, 2 * TILE :] = p2
                attn = dot(jnp.concatenate([p0, p1, p2], axis=1), v, 1, 0)
                attn_ref[i * TILE : (i + 1) * TILE, hcols] = attn.astype(BF16)


def forward(q, k, v, prev=None):
    first = prev is not None
    width = q.shape[1]
    kv_local = k.shape[1] // HEAD_SIZE
    group = width // k.shape[1]
    args = [q, k, v] + ([prev] if first else [])
    return pl.pallas_call(
        functools.partial(forward_kernel, kv_local, group, first),
        out_shape=[
            jax.ShapeDtypeStruct((WINDOW_KEYS, width), BF16),
            jax.ShapeDtypeStruct((kv_local, 2, group, TILE, 3 * TILE), BF16),
        ],
        in_specs=[vmem() for _ in args],
        out_specs=[vmem(), vmem()],
        compiler_params=params(),
        name="attention_forward_first" if first else "attention_forward_second",
    )(*args)


def backward_kernel(kv_local, group, first, *refs):
    q_ref, k_ref, v_ref, do_ref, attn_ref, prob_ref = refs[:6]
    if first:
        prev_ref, dq_ref, halo_ref, own_ref, dk_acc, dv_acc = refs[6:]
        base = 0
    else:
        low_ref, dq_ref, done_ref, own_ref, dk_acc, dv_acc = refs[6:]
        prev_ref = None
        base = q_ref.shape[0] - WINDOW_KEYS
    for g in range(kv_local):
        for i in range(2):
            rows = slice(i * TILE, (i + 1) * TILE)
            wide_rows = slice(base + i * TILE, base + (i + 1) * TILE)
            k = window(first, i, g, 0, prev_ref, k_ref)
            v = window(first, i, g, 1, prev_ref, v_ref)
            dk = jnp.zeros((HEAD_SIZE, 3 * TILE), F32)
            dv = jnp.zeros((HEAD_SIZE, 3 * TILE), F32)
            for h in range(group):
                head = g * group + h
                hcols = slice(head * HEAD_SIZE, (head + 1) * HEAD_SIZE)
                q = q_ref[wide_rows, hcols]
                do = do_ref[wide_rows, hcols]
                delta = jnp.sum(
                    do.astype(F32) * attn_ref[rows, hcols].astype(F32), axis=1, keepdims=True
                )
                p = prob_ref[g, i, h]
                ds = (p.astype(F32) * (dot(do, v, 1, 1) - delta)).astype(BF16)
                dq_ref[rows, hcols] = (dot(ds, k, 1, 0) * SCALE).astype(BF16)
                dk += dot(q, ds, 0, 0)
                dv += dot(do, p, 0, 0)
            if i == 0:
                dk_acc[:, : 3 * TILE] = dk
                dv_acc[:, : 3 * TILE] = dv
            else:
                dk_acc[:, TILE : 3 * TILE] += dk[:, : 2 * TILE]
                dv_acc[:, TILE : 3 * TILE] += dv[:, : 2 * TILE]
                dk_acc[:, 3 * TILE :] = dk[:, 2 * TILE :]
                dv_acc[:, 3 * TILE :] = dv[:, 2 * TILE :]
        cols = slice(g * HEAD_SIZE, (g + 1) * HEAD_SIZE)
        for which, acc, factor in ((0, dk_acc, SCALE), (1, dv_acc, 1.0)):
            low = acc[:, :WINDOW_KEYS].T
            high = acc[:, WINDOW_KEYS:].T
            if factor != 1.0:
                low, high = low * factor, high * factor
            if first:
                halo_ref[which, :, cols] = low.astype(BF16)
            else:
                done_ref[which, :, cols] = (low + low_ref[which, :, cols]).astype(BF16)
            own_ref[which, :, cols] = high


def backward(q, k, v, do, attn, prob, prev=None, low=None):
    first = prev is not None
    width = q.shape[1]
    kv_width = k.shape[1]
    args = [q, k, v, do, attn, prob, prev if first else low]
    return pl.pallas_call(
        functools.partial(backward_kernel, kv_width // HEAD_SIZE, width // kv_width, first),
        out_shape=[
            jax.ShapeDtypeStruct((WINDOW_KEYS, width), BF16),
            jax.ShapeDtypeStruct((2, WINDOW_KEYS, kv_width), BF16),
            jax.ShapeDtypeStruct((2, WINDOW_KEYS, kv_width), F32),
        ],
        in_specs=[vmem() for _ in args],
        out_specs=[vmem() for _ in range(3)],
        scratch_shapes=[
            pltpu.VMEM((HEAD_SIZE, 4 * TILE), F32),
            pltpu.VMEM((HEAD_SIZE, 4 * TILE), F32),
        ],
        compiler_params=params(),
        name="attention_backward_first" if first else "attention_backward_second",
    )(*args)


def join_kernel(done_ref, own_ref, got_ref, dk_ref, dv_ref):
    for which, out in ((0, dk_ref), (1, dv_ref)):
        rows = out.shape[0]
        out[: rows - WINDOW_KEYS, :] = done_ref[which]
        high = own_ref[which] + got_ref[which].astype(F32)
        out[rows - WINDOW_KEYS :, :] = high.astype(BF16)


def join(done, own, got, rows):
    shape = jax.ShapeDtypeStruct((rows, own.shape[2]), BF16)
    return pl.pallas_call(
        join_kernel,
        out_shape=[shape, shape],
        in_specs=[vmem()] * 3,
        out_specs=[vmem()] * 2,
        compiler_params=params(),
        name="join_gradients",
    )(done, own, got)


def concat_kernel(low_ref, high_ref, out_ref):
    rows = low_ref.shape[0]
    out_ref[:rows, :] = low_ref[...]
    out_ref[rows:, :] = high_ref[...]


def concat(low, high):
    return pl.pallas_call(
        concat_kernel,
        out_shape=jax.ShapeDtypeStruct((2 * low.shape[0], low.shape[1]), BF16),
        in_specs=[vmem()] * 2,
        out_specs=vmem(),
        compiler_params=params(),
        name="join_halves",
    )(low, high)


def add_kernel(parts, *refs):
    keep_refs, got_refs, out_refs = refs[:parts], refs[parts : 2 * parts], refs[2 * parts :]
    at = 0
    for keep_ref, got_ref in zip(keep_refs, got_refs):
        count, length = keep_ref.shape[:2]
        rows = slice(at, at + length)
        at += length
        for i in range(count):
            total = keep_ref[i].astype(F32) + got_ref[i].astype(F32)
            if count == 1:
                out_refs[0][rows, :] = total.astype(BF16)
            else:
                out = out_refs[i % 2]
                out[i // 2, rows, :] = total.astype(out.dtype)


def add(keeps, gots):
    count, _, width = keeps[0].shape
    length = sum(keep.shape[1] for keep in keeps)
    if count == 1:
        out_shape = [jax.ShapeDtypeStruct((length, width), BF16)]
    else:
        half = (count // 2, length, width)
        out_shape = [jax.ShapeDtypeStruct(half, F32), jax.ShapeDtypeStruct(half, BF16)]
    return pl.pallas_call(
        functools.partial(add_kernel, len(keeps)),
        out_shape=out_shape,
        in_specs=[vmem()] * (2 * len(keeps)),
        out_specs=[vmem() for _ in out_shape],
        compiler_params=params(),
        name="add_partials",
    )(*keeps, *gots)


def projection_kernel(peers, blocks, off, length, start, last, bits, *refs):
    og_refs = refs[:peers]
    w_ref, low_ref, high_ref = refs[peers : peers + 3]
    refs = refs[peers + 3 :]
    if not start:
        acc_ref, refs = refs[0], refs[1:]
    out_ref, keep_ref, send_ref, w_vmem, attn_all, part, sem = refs
    copy = pltpu.make_async_copy(w_ref.at[:, pl.ds(off, length), :], w_vmem, sem)
    copy.start()
    mine, context = lax.axis_index("mp"), lax.axis_index("context")
    rows, width = og_refs[0].shape[0], low_ref.shape[1]
    total = blocks * length
    for r in range(peers // 2):
        attn_all[r] = low_ref[r * rows : (r + 1) * rows, :]
        attn_all[r + peers // 2] = high_ref[r * rows : (r + 1) * rows, :]
    attn = jnp.concatenate([attn_all[mine ^ r] for r in range(peers)], axis=0)
    step = 256 if total % 256 == 0 else 128
    for s in range(0, total, step):
        og = jnp.concatenate([og_ref[:, s : s + step] for og_ref in og_refs], axis=0)
        part[s : s + step, :] = dot(og, attn, 0, 0)
    for i in range(blocks // 2):
        target = sum(bit for k, bit in enumerate(bits[1:]) if i >> k & 1) ^ context
        at = pl.multiple_of(target * length, 8)
        keep_ref[i] = part[pl.ds(at, length), :].astype(keep_ref.dtype)
        at = pl.multiple_of((target ^ bits[0]) * length, 8)
        send_ref[i] = part[pl.ds(at, length), :].astype(BF16)
    copy.wait()
    w = w_vmem[...].reshape(total, width)
    for r in range(peers):
        out = dot(og_refs[r][...], w, 1, 0)
        if not start:
            out = out + acc_ref[r]
        if last:
            out_ref[mine ^ r] = out.astype(BF16)
        else:
            out_ref[r] = out


def projection(ogs, w, low, high, acc, blocks, off, length, last, bits):
    peers = len(ogs)
    rows, total = ogs[0].shape
    width = low.shape[1]
    start = acc is None
    args = [*ogs, w, low, high] + ([] if start else [acc])
    specs = [vmem()] * peers + [hbm()] + [vmem()] * (2 if start else 3)
    half = jax.ShapeDtypeStruct((blocks // 2, length, width), BF16)
    return pl.pallas_call(
        functools.partial(
            projection_kernel, peers, blocks, off, length, start, last, bits
        ),
        out_shape=[
            jax.ShapeDtypeStruct((peers, rows, width), BF16 if last else F32),
            half,
            half,
        ],
        in_specs=specs,
        out_specs=[vmem()] * 3,
        scratch_shapes=[
            pltpu.VMEM((blocks, length, width), BF16),
            pltpu.VMEM((peers, rows, width), BF16),
            pltpu.VMEM((total, width), F32),
            pltpu.SemaphoreType.DMA,
        ],
        compiler_params=params(4 if start and last else 1),
        name="projection",
    )(*args)


def plan(blk, contexts):
    bits = [1 << k for k in range(contexts.bit_length() - 1)]
    if blk == 672 and contexts == 8:
        groups = [[[chunk] for chunk in range(len(LENS))]] * len(bits)
        return LENS, [bits] * len(LENS), groups, STEPS
    groups = [[[0]]] * len(bits)
    steps = ["y0", "p0", "first", "second"] + [f"{k + 1}.0" for k in range(len(bits))]
    return (blk,), [bits], groups, steps


def exchange(x, axis, by):
    return lax.ppermute(x, axis, [(i, i ^ by) for i in range(lax.axis_size(axis))])


def after(done, x):
    return lax.optimization_barrier((x, done))[0]


def shards(queries, keys, values, out_grad, out_weight):
    shard, width = queries.shape
    contexts = lax.axis_size("context")
    peers = lax.axis_size("mp")
    blk = out_weight.shape[0] // contexts
    lens, orders, groups, steps = plan(blk, contexts)
    chunks = len(lens)
    weight = out_weight.reshape(contexts, blk, width)

    own = prepare(out_grad, contexts, lens)
    halo = pack(after(own[0], keys), values)
    sibling = exchange(out_grad, "mp", 1)
    far = [[exchange(og, "mp", by) for by in range(2, peers, 2)] for og in own]
    halo = lax.ppermute(halo, "context", [(i, i + 1) for i in range(contexts - 1)])

    attn_high, prob_high = forward(queries, keys, values)
    siblings = prepare(after(attn_high, sibling), contexts, lens)
    halo = after(siblings[0], halo)
    attn_low, prob_low = forward(queries, keys, values, halo)
    done = attn_low

    stages = len(orders[0])
    fetched, item, grads = {}, {}, {}
    acc, offs = None, [sum(lens[:j]) for j in range(chunks)]
    for step in steps:
        if step[0] == "y":
            theirs = [after(done, og) for og in far[int(step[1:])]]
            fetched[int(step[1:])] = theirs, [exchange(og, "mp", 1) for og in theirs]
            done = theirs[-1]
        elif step[0] == "p":
            j = int(step[1:])
            parts = [own[j], after(done, siblings[j])]
            for og, og_sibling in zip(*fetched[j]):
                parts += [og, after(done, og_sibling)]
            acc, keep, send = projection(
                parts, weight, attn_low, attn_high, acc, contexts, offs[j], lens[j],
                j == chunks - 1, orders[j],
            )
            item[0, j] = keep, exchange(send, "context", orders[j][0]), orders[j]
            done = acc
        elif step == "first":
            dout = acc.reshape(shard, width)
            dq_low, halo_grad, own_low = backward(
                queries, keys, values, after(done, dout), attn_low, prob_low, halo
            )
            pairs = [(i + 1, i) for i in range(contexts - 1)]
            halo_grad = lax.ppermute(halo_grad, "context", pairs)
            done = own_low
        elif step == "second":
            dq_high, kv_low, own_high = backward(
                queries, keys, values, after(done, dout), attn_high, prob_high, low=own_low
            )
            done = own_high
        elif step == "halves":
            dq = concat(after(done, dq_low), dq_high)
            done = dq
        elif step == "join":
            dk, dv = join(kv_low, own_high, after(done, halo_grad), shard)
            done = dk
        else:
            stage, group = [int(n) for n in step.split(".")]
            members = [item[stage - 1, g] for g in groups[stage - 1][group]]
            keeps, gots = [m[0] for m in members], [after(done, m[1]) for m in members]
            order = members[0][2]
            if stage == stages:
                item[stage, group] = done = add(keeps, gots)[0]
            else:
                keep, done = add(keeps, gots)
                item[stage, group] = keep, exchange(done, "context", order[stage]), order
    final = [item[stages, g] for g in range(len(groups[-1]))]
    weight_grad = final[0] if len(final) == 1 else jnp.concatenate(final, axis=0)
    if "halves" not in steps:
        dq = concat(dq_low, dq_high)
    if "join" not in steps:
        dk, dv = join(kv_low, own_high, halo_grad, shard)
    return dq, dk, dv, weight_grad


def solution(mesh):
    return jax.shard_map(
        shards,
        mesh=mesh,
        in_specs=(
            P("context", "mp"),
            P("context", "mp"),
            P("context", "mp"),
            P(("context", "mp"), None),
            P(None, "mp"),
        ),
        out_specs=(P("context", "mp"), P("context", "mp"), P("context", "mp"), P("context", "mp")),
        check_vma=False,
    )
```

```python
import functools

import jax
import jax.numpy as jnp
from jax import lax
from jax.experimental import pallas as pl
from jax.experimental.pallas import tpu as pltpu
from jax.sharding import PartitionSpec as P

HEAD_SIZE = 128
WINDOW_KEYS = 512
SCALE = 168.0 ** (-0.5)
LOG2E = 1.4426950408889634
NEG = -1e30
TILE = WINDOW_KEYS // 2
LENS = (144, 144, 128, 112, 80, 64)
STEPS = (
    "y0", "y1", "p0", "y2", "p1", "1.0", "y3", "p2", "2.0", "1.1", "y4", "3.0", "p3",
    "2.1", "1.2", "y5", "p4", "p5", "3.1", "1.3", "2.2", "first", "3.2", "2.3", "1.4",
    "second", "1.5", "2.4", "3.3", "2.5", "3.4", "3.5",
)
F32 = jnp.float32
BF16 = jnp.bfloat16
VMEM_LIMIT = 8 * 1024 * 1024


def dot(a, b, contract_a, contract_b):
    return lax.dot_general(
        a, b, (((contract_a,), (contract_b,)), ((), ())), preferred_element_type=F32
    )


def vmem():
    return pl.BlockSpec(memory_space=pltpu.VMEM)


def hbm():
    return pl.BlockSpec(memory_space=pltpu.HBM)


def params(times=1):
    return pltpu.CompilerParams(vmem_limit_bytes=times * VMEM_LIMIT)


def prepare_kernel(blocks, blk, lens, og_ref, *refs):
    *out_refs, rows_vmem, sems = refs
    size = og_ref.shape[0] // 4
    copies = []
    for n in range(4):
        rows = pl.ds(n * size, size)
        copies.append(
            pltpu.make_async_copy(og_ref.at[rows, :], rows_vmem.at[rows, :], sems.at[n])
        )
        copies[-1].start()
    for n, copy in enumerate(copies):
        copy.wait()
        rows = slice(n * size, (n + 1) * size)
        off = 0
        for out, length in zip(out_refs, lens):
            at = [t * blk + off for t in range(blocks)]
            out[rows, :] = jnp.concatenate(
                [rows_vmem[rows, start : start + length] for start in at], axis=1
            )
            off += length


def prepare(og, blocks, lens):
    rows, width = og.shape
    return pl.pallas_call(
        functools.partial(prepare_kernel, blocks, width // blocks, lens),
        out_shape=[jax.ShapeDtypeStruct((rows, blocks * n), BF16) for n in lens],
        in_specs=[hbm()],
        out_specs=[vmem() for _ in lens],
        scratch_shapes=[pltpu.VMEM((rows, width), BF16), pltpu.SemaphoreType.DMA((4,))],
        compiler_params=params(),
        name="gather_columns",
    )(og)


def pack_kernel(k_ref, v_ref, out_ref):
    rows = k_ref.shape[0]
    out_ref[0] = k_ref[rows - WINDOW_KEYS :, :]
    out_ref[1] = v_ref[rows - WINDOW_KEYS :, :]


def pack(keys, values):
    return pl.pallas_call(
        pack_kernel,
        out_shape=jax.ShapeDtypeStruct((2, WINDOW_KEYS, keys.shape[1]), BF16),
        in_specs=[vmem(), vmem()],
        out_specs=vmem(),
        compiler_params=params(),
        name="pack_halo",
    )(keys, values)


def window(first, i, g, which, prev_ref, own_ref):
    cols = slice(g * HEAD_SIZE, (g + 1) * HEAD_SIZE)
    start = i * TILE
    if not first:
        return own_ref[start : start + 3 * TILE, cols]
    low = prev_ref[which, start:, cols]
    return jnp.concatenate([low, own_ref[: start + TILE, cols]], axis=0)


def forward_kernel(kv_local, group, first, *refs):
    if first:
        q_ref, k_ref, v_ref, prev_ref, attn_ref, prob_ref = refs
        has_prev = lax.axis_index("context") > 0
        base = 0
    else:
        q_ref, k_ref, v_ref, attn_ref, prob_ref = refs
        prev_ref = None
        base = q_ref.shape[0] - WINDOW_KEYS
    row = lax.broadcasted_iota(jnp.int32, (TILE, TILE), 0)
    col = lax.broadcasted_iota(jnp.int32, (TILE, TILE), 1)
    upper = col > row
    for g in range(kv_local):
        for i in range(2):
            k = window(first, i, g, 0, prev_ref, k_ref)
            v = window(first, i, g, 1, prev_ref, v_ref)
            for h in range(group):
                head = g * group + h
                hcols = slice(head * HEAD_SIZE, (head + 1) * HEAD_SIZE)
                q = q_ref[base + i * TILE : base + (i + 1) * TILE, hcols]
                s = dot(q, k, 1, 1)
                s0, s1, s2 = s[:, :TILE], s[:, TILE : 2 * TILE], s[:, 2 * TILE :]
                if first:
                    s0 = jnp.where(has_prev, s0, NEG)
                    if i == 0:
                        s1 = jnp.where(has_prev, s1, NEG)
                edge = jnp.where(upper, s0, s2)
                top = jnp.max(jnp.maximum(edge, s1), axis=1, keepdims=True)
                edge = jnp.exp2((edge - top) * (SCALE * LOG2E))
                mid = jnp.exp2((s1 - top) * (SCALE * LOG2E))
                inv = 1.0 / jnp.sum(edge + mid, axis=1, keepdims=True)
                edge = edge * inv
                p0 = jnp.where(upper, edge, 0.0).astype(BF16)
                p1 = (mid * inv).astype(BF16)
                p2 = jnp.where(upper, 0.0, edge).astype(BF16)
                prob_ref[g, i, h, :, :TILE] = p0
                prob_ref[g, i, h, :, TILE : 2 * TILE] = p1
                prob_ref[g, i, h, :, 2 * TILE :] = p2
                attn = dot(jnp.concatenate([p0, p1, p2], axis=1), v, 1, 0)
                attn_ref[i * TILE : (i + 1) * TILE, hcols] = attn.astype(BF16)


def forward(q, k, v, prev=None):
    first = prev is not None
    width = q.shape[1]
    kv_local = k.shape[1] // HEAD_SIZE
    group = width // k.shape[1]
    args = [q, k, v] + ([prev] if first else [])
    return pl.pallas_call(
        functools.partial(forward_kernel, kv_local, group, first),
        out_shape=[
            jax.ShapeDtypeStruct((WINDOW_KEYS, width), BF16),
            jax.ShapeDtypeStruct((kv_local, 2, group, TILE, 3 * TILE), BF16),
        ],
        in_specs=[vmem() for _ in args],
        out_specs=[vmem(), vmem()],
        compiler_params=params(),
        name="attention_forward_first" if first else "attention_forward_second",
    )(*args)


def backward_kernel(kv_local, group, first, *refs):
    q_ref, k_ref, v_ref, do_ref, attn_ref, prob_ref = refs[:6]
    if first:
        prev_ref, dq_ref, halo_ref, own_ref, dk_acc, dv_acc = refs[6:]
        base = 0
    else:
        low_ref, dq_ref, done_ref, own_ref, dk_acc, dv_acc = refs[6:]
        prev_ref = None
        base = q_ref.shape[0] - WINDOW_KEYS
    for g in range(kv_local):
        for i in range(2):
            rows = slice(i * TILE, (i + 1) * TILE)
            wide_rows = slice(base + i * TILE, base + (i + 1) * TILE)
            k = window(first, i, g, 0, prev_ref, k_ref)
            v = window(first, i, g, 1, prev_ref, v_ref)
            dk = jnp.zeros((HEAD_SIZE, 3 * TILE), F32)
            dv = jnp.zeros((HEAD_SIZE, 3 * TILE), F32)
            for h in range(group):
                head = g * group + h
                hcols = slice(head * HEAD_SIZE, (head + 1) * HEAD_SIZE)
                q = q_ref[wide_rows, hcols]
                do = do_ref[wide_rows, hcols]
                delta = jnp.sum(
                    do.astype(F32) * attn_ref[rows, hcols].astype(F32), axis=1, keepdims=True
                )
                p = prob_ref[g, i, h]
                ds = (p.astype(F32) * (dot(do, v, 1, 1) - delta)).astype(BF16)
                dq_ref[rows, hcols] = (dot(ds, k, 1, 0) * SCALE).astype(BF16)
                dk += dot(q, ds, 0, 0)
                dv += dot(do, p, 0, 0)
            if i == 0:
                dk_acc[:, : 3 * TILE] = dk
                dv_acc[:, : 3 * TILE] = dv
            else:
                dk_acc[:, TILE : 3 * TILE] += dk[:, : 2 * TILE]
                dv_acc[:, TILE : 3 * TILE] += dv[:, : 2 * TILE]
                dk_acc[:, 3 * TILE :] = dk[:, 2 * TILE :]
                dv_acc[:, 3 * TILE :] = dv[:, 2 * TILE :]
        cols = slice(g * HEAD_SIZE, (g + 1) * HEAD_SIZE)
        for which, acc, factor in ((0, dk_acc, SCALE), (1, dv_acc, 1.0)):
            low = acc[:, :WINDOW_KEYS].T
            high = acc[:, WINDOW_KEYS:].T
            if factor != 1.0:
                low, high = low * factor, high * factor
            if first:
                halo_ref[which, :, cols] = low.astype(BF16)
            else:
                done_ref[which, :, cols] = (low + low_ref[which, :, cols]).astype(BF16)
            own_ref[which, :, cols] = high


def backward(q, k, v, do, attn, prob, prev=None, low=None):
    first = prev is not None
    width = q.shape[1]
    kv_width = k.shape[1]
    args = [q, k, v, do, attn, prob, prev if first else low]
    return pl.pallas_call(
        functools.partial(backward_kernel, kv_width // HEAD_SIZE, width // kv_width, first),
        out_shape=[
            jax.ShapeDtypeStruct((WINDOW_KEYS, width), BF16),
            jax.ShapeDtypeStruct((2, WINDOW_KEYS, kv_width), BF16),
            jax.ShapeDtypeStruct((2, WINDOW_KEYS, kv_width), F32),
        ],
        in_specs=[vmem() for _ in args],
        out_specs=[vmem() for _ in range(3)],
        scratch_shapes=[
            pltpu.VMEM((HEAD_SIZE, 4 * TILE), F32),
            pltpu.VMEM((HEAD_SIZE, 4 * TILE), F32),
        ],
        compiler_params=params(),
        name="attention_backward_first" if first else "attention_backward_second",
    )(*args)


def join_kernel(done_ref, own_ref, got_ref, dk_ref, dv_ref):
    for which, out in ((0, dk_ref), (1, dv_ref)):
        rows = out.shape[0]
        out[: rows - WINDOW_KEYS, :] = done_ref[which]
        high = own_ref[which] + got_ref[which].astype(F32)
        out[rows - WINDOW_KEYS :, :] = high.astype(BF16)


def join(done, own, got, rows):
    shape = jax.ShapeDtypeStruct((rows, own.shape[2]), BF16)
    return pl.pallas_call(
        join_kernel,
        out_shape=[shape, shape],
        in_specs=[vmem()] * 3,
        out_specs=[vmem()] * 2,
        compiler_params=params(),
        name="join_gradients",
    )(done, own, got)


def concat_kernel(low_ref, high_ref, out_ref):
    rows = low_ref.shape[0]
    out_ref[:rows, :] = low_ref[...]
    out_ref[rows:, :] = high_ref[...]


def concat(low, high):
    return pl.pallas_call(
        concat_kernel,
        out_shape=jax.ShapeDtypeStruct((2 * low.shape[0], low.shape[1]), BF16),
        in_specs=[vmem()] * 2,
        out_specs=vmem(),
        compiler_params=params(),
        name="join_halves",
    )(low, high)


def add_kernel(parts, *refs):
    keep_refs, got_refs, out_refs = refs[:parts], refs[parts : 2 * parts], refs[2 * parts :]
    at = 0
    for keep_ref, got_ref in zip(keep_refs, got_refs):
        count, length = keep_ref.shape[:2]
        rows = slice(at, at + length)
        at += length
        for i in range(count):
            total = keep_ref[i].astype(F32) + got_ref[i].astype(F32)
            if count == 1:
                out_refs[0][rows, :] = total.astype(BF16)
            else:
                out = out_refs[i % 2]
                out[i // 2, rows, :] = total.astype(out.dtype)


def add(keeps, gots):
    count, _, width = keeps[0].shape
    length = sum(keep.shape[1] for keep in keeps)
    if count == 1:
        out_shape = [jax.ShapeDtypeStruct((length, width), BF16)]
    else:
        half = (count // 2, length, width)
        out_shape = [jax.ShapeDtypeStruct(half, F32), jax.ShapeDtypeStruct(half, BF16)]
    return pl.pallas_call(
        functools.partial(add_kernel, len(keeps)),
        out_shape=out_shape,
        in_specs=[vmem()] * (2 * len(keeps)),
        out_specs=[vmem() for _ in out_shape],
        compiler_params=params(),
        name="add_partials",
    )(*keeps, *gots)


def projection_kernel(peers, blocks, off, length, start, last, bits, *refs):
    og_refs = refs[:peers]
    w_ref, low_ref, high_ref = refs[peers : peers + 3]
    refs = refs[peers + 3 :]
    if not start:
        acc_ref, refs = refs[0], refs[1:]
    out_ref, keep_ref, send_ref, w_vmem, attn_all, part, sem = refs
    copy = pltpu.make_async_copy(w_ref.at[:, pl.ds(off, length), :], w_vmem, sem)
    copy.start()
    mine, context = lax.axis_index("mp"), lax.axis_index("context")
    rows, width = og_refs[0].shape[0], low_ref.shape[1]
    total = blocks * length
    for r in range(peers // 2):
        attn_all[r] = low_ref[r * rows : (r + 1) * rows, :]
        attn_all[r + peers // 2] = high_ref[r * rows : (r + 1) * rows, :]
    attn = jnp.concatenate([attn_all[mine ^ r] for r in range(peers)], axis=0)
    step = 256 if total % 256 == 0 else 128
    for s in range(0, total, step):
        og = jnp.concatenate([og_ref[:, s : s + step] for og_ref in og_refs], axis=0)
        part[s : s + step, :] = dot(og, attn, 0, 0)
    for i in range(blocks // 2):
        target = sum(bit for k, bit in enumerate(bits[1:]) if i >> k & 1) ^ context
        at = pl.multiple_of(target * length, 8)
        keep_ref[i] = part[pl.ds(at, length), :].astype(keep_ref.dtype)
        at = pl.multiple_of((target ^ bits[0]) * length, 8)
        send_ref[i] = part[pl.ds(at, length), :].astype(BF16)
    copy.wait()
    w = w_vmem[...].reshape(total, width)
    for r in range(peers):
        out = dot(og_refs[r][...], w, 1, 0)
        if not start:
            out = out + acc_ref[r]
        if last:
            out_ref[mine ^ r] = out.astype(BF16)
        else:
            out_ref[r] = out


def projection(ogs, w, low, high, acc, blocks, off, length, last, bits):
    peers = len(ogs)
    rows, total = ogs[0].shape
    width = low.shape[1]
    start = acc is None
    args = [*ogs, w, low, high] + ([] if start else [acc])
    specs = [vmem()] * peers + [hbm()] + [vmem()] * (2 if start else 3)
    half = jax.ShapeDtypeStruct((blocks // 2, length, width), BF16)
    return pl.pallas_call(
        functools.partial(
            projection_kernel, peers, blocks, off, length, start, last, bits
        ),
        out_shape=[
            jax.ShapeDtypeStruct((peers, rows, width), BF16 if last else F32),
            half,
            half,
        ],
        in_specs=specs,
        out_specs=[vmem()] * 3,
        scratch_shapes=[
            pltpu.VMEM((blocks, length, width), BF16),
            pltpu.VMEM((peers, rows, width), BF16),
            pltpu.VMEM((total, width), F32),
            pltpu.SemaphoreType.DMA,
        ],
        compiler_params=params(4 if start and last else 1),
        name="projection",
    )(*args)


def plan(blk, contexts):
    bits = [1 << k for k in range(contexts.bit_length() - 1)]
    if blk == 672 and contexts == 8:
        groups = [[[chunk] for chunk in range(len(LENS))]] * len(bits)
        return LENS, [bits] * len(LENS), groups, STEPS
    groups = [[[0]]] * len(bits)
    steps = ["y0", "p0", "first", "second"] + [f"{k + 1}.0" for k in range(len(bits))]
    return (blk,), [bits], groups, steps


def exchange(x, axis, by):
    return lax.ppermute(x, axis, [(i, i ^ by) for i in range(lax.axis_size(axis))])


def after(done, x):
    return lax.optimization_barrier((x, done))[0]


def shards(queries, keys, values, out_grad, out_weight):
    shard, width = queries.shape
    contexts = lax.axis_size("context")
    peers = lax.axis_size("mp")
    blk = out_weight.shape[0] // contexts
    lens, orders, groups, steps = plan(blk, contexts)
    chunks = len(lens)
    weight = out_weight.reshape(contexts, blk, width)

    own = prepare(out_grad, contexts, lens)
    halo = pack(after(own[0], keys), values)
    sibling = exchange(out_grad, "mp", 1)
    far = [[exchange(og, "mp", by) for by in range(2, peers, 2)] for og in own]
    halo = lax.ppermute(halo, "context", [(i, i + 1) for i in range(contexts - 1)])

    attn_high, prob_high = forward(queries, keys, values)
    siblings = prepare(after(attn_high, sibling), contexts, lens)
    halo = after(siblings[0], halo)
    attn_low, prob_low = forward(queries, keys, values, halo)
    done = attn_low

    stages = len(orders[0])
    fetched, item, grads = {}, {}, {}
    acc, offs = None, [sum(lens[:j]) for j in range(chunks)]
    for step in steps:
        if step[0] == "y":
            theirs = [after(done, og) for og in far[int(step[1:])]]
            fetched[int(step[1:])] = theirs, [exchange(og, "mp", 1) for og in theirs]
            done = theirs[-1]
        elif step[0] == "p":
            j = int(step[1:])
            parts = [own[j], after(done, siblings[j])]
            for og, og_sibling in zip(*fetched[j]):
                parts += [og, after(done, og_sibling)]
            acc, keep, send = projection(
                parts, weight, attn_low, attn_high, acc, contexts, offs[j], lens[j],
                j == chunks - 1, orders[j],
            )
            item[0, j] = keep, exchange(send, "context", orders[j][0]), orders[j]
            done = acc
        elif step == "first":
            dout = acc.reshape(shard, width)
            dq_low, halo_grad, own_low = backward(
                queries, keys, values, after(done, dout), attn_low, prob_low, halo
            )
            pairs = [(i + 1, i) for i in range(contexts - 1)]
            halo_grad = lax.ppermute(halo_grad, "context", pairs)
            done = own_low
        elif step == "second":
            dq_high, kv_low, own_high = backward(
                queries, keys, values, after(done, dout), attn_high, prob_high, low=own_low
            )
            done = own_high
        elif step == "halves":
            dq = concat(after(done, dq_low), dq_high)
            done = dq
        elif step == "join":
            dk, dv = join(kv_low, own_high, after(done, halo_grad), shard)
            done = dk
        else:
            stage, group = [int(n) for n in step.split(".")]
            members = [item[stage - 1, g] for g in groups[stage - 1][group]]
            keeps, gots = [m[0] for m in members], [after(done, m[1]) for m in members]
            order = members[0][2]
            if stage == stages:
                item[stage, group] = done = add(keeps, gots)[0]
            else:
                keep, done = add(keeps, gots)
                item[stage, group] = keep, exchange(done, "context", order[stage]), order
    final = [item[stages, g] for g in range(len(groups[-1]))]
    weight_grad = final[0] if len(final) == 1 else jnp.concatenate(final, axis=0)
    if "halves" not in steps:
        dq = concat(dq_low, dq_high)
    if "join" not in steps:
        dk, dv = join(kv_low, own_high, halo_grad, shard)
    return dq, dk, dv, weight_grad


def solution(mesh):
    return jax.shard_map(
        shards,
        mesh=mesh,
        in_specs=(
            P("context", "mp"),
            P("context", "mp"),
            P("context", "mp"),
            P(("context", "mp"), None),
            P(None, "mp"),
        ),
        out_specs=(P("context", "mp"), P("context", "mp"), P("context", "mp"), P("context", "mp")),
        check_vma=False,
    )
```
